32 devices in a mesh: segment: 4 (over y, x), fsdp: 4 (over z), rep: 2 (over core).
Axes of the slice: x: 2, y: 2, z: 4, core: 2. Of those that a mesh axis runs over, the one named last changes fastest.
Arguments:
- token_ids: int32 [32, 128], P('fsdp'), may hold values from 0 to 127
- seq_lengths: int32 [32], P('fsdp'), may hold values from 32 to 128, as said below
- quant_scores: int32 [32], P('fsdp'), may hold values from 0 to 64
- embed_table: bfloat16 [128, 4096], replicated, may hold values from -6 to 6
- prior_weight: bfloat16 [4, 4096, 4096], P('segment', None, 'rep'), may hold values from -0.09375 to 0.09375
- prior_gain: float32 [4, 4096], P('segment'), may hold values from 0.25 to 1.75
- final_gain: float32 [4096], replicated, may hold values from 0.25 to 1.75
- head_weight: bfloat16 [4096, 128], replicated, may hold values from -0.25 to 0.25
- agent_down: bfloat16 [4096, 256], P('fsdp'), may hold values from -0.09375 to 0.09375
- agent_up: bfloat16 [4096, 256], P('fsdp'), may hold values from -0.375 to 0.375
Outputs:
- down_gradient: float32 [4096, 256], P(('segment', 'fsdp', 'rep'))
- up_gradient: float32 [4096, 256], P(('segment', 'fsdp', 'rep'))
The draws below stay inside these ranges and needn't reach their ends.
Inputs may be any that keep to these rules, and one draw needn't show every extreme that they name: `seq_lengths`: every sequence keeps at least 32 tokens, and some sequence in every draw has all 128.
All inputs are finite; a program needn't handle non-finite values.
Results may differ from the reference program's by a relative error of at most 0.0081.
Values may be sent and summed in bfloat16 or wider, within the bound.
A program may use at most 128 MiB of HBM per device.

```python
import jax
import jax.numpy as jnp
from jax import lax

D = 4096
V = 128
R = 256
L = 128
LEVELS = 64
SEQS = 32
N_SEGMENT = 4


def draw_seq_lengths(key, part):
    values = jax.random.randint(key, (SEQS,), L // 4, L + 1)
    return values.at[0].set(L).astype(jnp.int32)


def place_ends(result, own_key, smallest, high):
    spot = [jax.random.randint(jax.random.fold_in(own_key, axis), (), 0, length) for axis, length in enumerate(result.shape)]
    widest = result.shape.index(max(result.shape))
    beside = spot[:widest] + [(spot[widest] + 1) % result.shape[widest]] + spot[widest + 1:]
    return result.at[tuple(spot)].set(smallest).at[tuple(beside)].set(high)


def steps_of(key, extent, split, smallest, largest):
    factor_of = 1.0
    for dim, shards_of in split:
        draws = jax.random.uniform(jax.random.fold_in(jax.random.fold_in(key, 6), dim), (shards_of,), jnp.float32, smallest / len(split), largest / len(split))
        factor_of = factor_of * jnp.repeat(jnp.exp(draws), extent[dim] // shards_of).reshape((-1,) + (1,) * (len(extent) - 1 - dim))
    return factor_of


def centred(own_key, shape, spread, bound, cuts=(), kind=jnp.bfloat16):
    values = jax.random.normal(own_key, shape, jnp.float32) * spread
    if len(cuts) > 0:
        values = steps_of(own_key, shape, cuts, -0.22, 0.18) * values
    return jnp.clip(values, min=-bound, max=bound).astype(kind)


def setup_inputs(seed: int = 0) -> dict:
    keys = jax.random.split(jax.random.key(seed), 11)
    return {
        "token_ids": place_ends(jax.random.randint(keys[0], (SEQS, L), 0, V), jax.random.fold_in(keys[0], 1), 0, V - 1).astype(jnp.int32),
        "seq_lengths": draw_seq_lengths(jax.random.fold_in(keys[10], 71), 0),
        "quant_scores": place_ends(jax.random.randint(keys[2], (SEQS,), 0, LEVELS + 1), jax.random.fold_in(keys[2], 1), 0, LEVELS).astype(jnp.int32),
        "embed_table": centred(keys[3], (V, D), 1.0, 6.0),
        "prior_weight": centred(keys[4], (N_SEGMENT, D, D), D ** -0.5, 0.09375, ((0, 4), (2, 2))),
        "prior_gain": jnp.clip(1.0 + 0.15 * jax.random.normal(keys[5], (N_SEGMENT, D), jnp.float32), 0.25, 1.75),
        "final_gain": jnp.clip(1.0 + 0.15 * jax.random.normal(keys[6], (D,), jnp.float32), 0.25, 1.75),
        "head_weight": centred(keys[7], (D, V), (D // 9) ** -0.5, 0.25),
        "agent_down": centred(keys[8], (D, R), D ** -0.5, 0.09375, ((0, 4),)),
        "agent_up": centred(keys[9], (D, R), R ** -0.5, 0.375, ((0, 4),)),
    }


epsilon = 1e-05
sigma_weight = 2.0

def rms_scale(values):
    squares = lax.optimization_barrier(jnp.mean(values * values, axis=-1, keepdims=True))
    return lax.rsqrt(squares + epsilon)

def picked_logprob(logprob, targets):
    vocab_size = logprob.shape[-1]
    column = jnp.arange(vocab_size, dtype=jnp.int32)
    return lax.optimization_barrier(jnp.sum(jnp.where(column[None, :] == targets[:, None], logprob, 0.0), axis=-1))

def reference(token_ids, seq_lengths, quant_scores, embed_table, prior_weight, prior_gain, final_gain, head_weight, agent_down, agent_up):
    seq_total, seq_len = token_ids.shape
    vocab_size = embed_table.shape[0]
    flat_ids = token_ids.reshape(-1)
    next_ids = jnp.concatenate([token_ids[:, 1:], token_ids[:, :1]], axis=1).reshape(-1)
    positions = jnp.arange(seq_len, dtype=jnp.int32)
    live_mask = (positions[None, :] < seq_lengths[:, None] - 1).astype(jnp.float32)
    counts = (seq_lengths - 1).astype(jnp.float32)
    start_rows = jnp.take(embed_table, flat_ids, axis=0)
    rows_now = start_rows
    for segment_pos in range(N_SEGMENT):
        wide_rows = rows_now.astype(jnp.float32)
        normed = (wide_rows * rms_scale(wide_rows) * prior_gain[segment_pos]).astype(jnp.bfloat16)
        update = jnp.dot(normed, prior_weight[segment_pos], preferred_element_type=jnp.float32)
        rows_now = (wide_rows + update).astype(jnp.bfloat16)
    final_wide = rows_now.astype(jnp.float32)
    prior_final = (final_wide * rms_scale(final_wide) * final_gain).astype(jnp.bfloat16)
    prior_logp = jax.nn.log_softmax(jnp.dot(prior_final, head_weight, preferred_element_type=jnp.float32), axis=-1)
    prior_ll = lax.optimization_barrier(jnp.sum(picked_logprob(prior_logp, next_ids).reshape(seq_total, seq_len) * live_mask, axis=1)) / counts
    start_wide = start_rows.astype(jnp.float32)
    unit_rows = (start_wide * rms_scale(start_wide)).astype(jnp.bfloat16)
    latent = jnp.dot(unit_rows, agent_down, preferred_element_type=jnp.float32).astype(jnp.bfloat16)
    hidden = start_wide + jnp.dot(latent, agent_up.T, preferred_element_type=jnp.float32)
    inverse = rms_scale(hidden)
    agent_final = (hidden * inverse * final_gain).astype(jnp.bfloat16)
    agent_logp = jax.nn.log_softmax(jnp.dot(agent_final, head_weight, preferred_element_type=jnp.float32), axis=-1)
    agent_ll = lax.optimization_barrier(jnp.sum(picked_logprob(agent_logp, next_ids).reshape(seq_total, seq_len) * live_mask, axis=1)) / counts
    margin = prior_ll + sigma_weight * quant_scores.astype(jnp.float32) / LEVELS - agent_ll
    row_factor = ((2.0 * margin / counts)[:, None] * live_mask).reshape(-1)
    column = jnp.arange(vocab_size, dtype=jnp.int32)
    onehot_next = (next_ids[:, None] == column[None, :]).astype(jnp.float32)
    logit_grad = (row_factor[:, None] * (jnp.exp(agent_logp) - onehot_next)).astype(jnp.bfloat16)
    scaled_grad = jnp.dot(logit_grad, head_weight.T, preferred_element_type=jnp.float32) * final_gain
    hidden_grad = (inverse * scaled_grad - hidden * inverse * inverse * inverse * lax.optimization_barrier(jnp.mean(hidden * scaled_grad, axis=-1, keepdims=True))).astype(jnp.bfloat16)
    up_gradient = jnp.dot(hidden_grad.T, latent, preferred_element_type=jnp.float32)
    latent_grad = jnp.dot(hidden_grad, agent_up, preferred_element_type=jnp.float32).astype(jnp.bfloat16)
    down_gradient = jnp.dot(unit_rows.T, latent_grad, preferred_element_type=jnp.float32)
    return (down_gradient, up_gradient)
```

```python
import jax
import jax.numpy as jnp
from jax import lax
from jax.sharding import PartitionSpec as P

LEVELS = 64
EPSILON = 1e-05
SIGMA_WEIGHT = 2.0

bf16 = jnp.bfloat16
f32 = jnp.float32


def rms_scale(values):
    squares = jnp.mean(values * values, axis=-1, keepdims=True)
    return lax.rsqrt(squares + EPSILON)


def dot(a, b, dims):
    return lax.dot_general(a, b, (dims, ((), ())), preferred_element_type=f32)


def on_device(
    token_ids,
    seq_lengths,
    quant_scores,
    embed_table,
    prior_weight,
    prior_gain,
    final_gain,
    head_weight,
    agent_down,
    agent_up,
):
    segments = lax.axis_size("segment")
    groups = lax.axis_size("fsdp")
    replicas = lax.axis_size("rep")
    segment_pos = lax.axis_index("segment")
    group_pos = lax.axis_index("fsdp")
    rep_pos = lax.axis_index("rep")
    vocab, width = embed_table.shape
    half = prior_weight.shape[2]
    seq_len = token_ids.shape[1]
    weight = prior_weight[0]
    gain = prior_gain[0]
    own_rows = vocab // groups

    rows = lax.dynamic_slice_in_dim(embed_table, group_pos * own_rows, own_rows, 0)
    pairs = [(i, i + 1) for i in range(segments - 1)]
    for s in range(segments):
        wide = rows.astype(f32)
        normed = (wide * rms_scale(wide) * gain).astype(bf16)
        update = dot(normed, weight, ((1,), (0,)))
        own = lax.dynamic_slice_in_dim(wide, rep_pos * half, half, 1)
        part = (own + update).astype(bf16)
        rows = lax.all_gather(part, "rep", axis=1, tiled=True)
        if s < segments - 1:
            rows = lax.ppermute(rows, "segment", pairs)
    wide = rows.astype(f32)
    prior_final = (wide * rms_scale(wide) * final_gain).astype(bf16)
    prior_part = jax.nn.log_softmax(dot(prior_final, head_weight, ((1,), (0,))), axis=-1)
    prior_part = jnp.where(segment_pos == segments - 1, prior_part, 0.0)
    slot = jnp.zeros((vocab, vocab), f32)
    slot = lax.dynamic_update_slice_in_dim(slot, prior_part, group_pos * own_rows, 0)
    prior_logp = lax.psum(slot, ("segment", "fsdp"))

    ids = lax.all_gather(token_ids, "fsdp", axis=0, tiled=True)
    lengths = lax.all_gather(seq_lengths, "fsdp", axis=0, tiled=True)
    scores = lax.all_gather(quant_scores, "fsdp", axis=0, tiled=True)
    down = lax.all_gather(agent_down, "fsdp", axis=0, tiled=True)
    up = lax.all_gather(agent_up, "fsdp", axis=0, tiled=True)
    start = embed_table.astype(f32)
    unit = (start * rms_scale(start)).astype(bf16)
    latent = dot(unit, down, ((1,), (0,))).astype(bf16)
    hidden = start + dot(latent, up, ((1,), (1,)))
    inverse = rms_scale(hidden)
    agent_final = (hidden * inverse * final_gain).astype(bf16)
    agent_logp = jax.nn.log_softmax(dot(agent_final, head_weight, ((1,), (0,))), axis=-1)

    seqs = ids.shape[0]
    next_ids = jnp.concatenate([ids[:, 1:], ids[:, :1]], axis=1)
    live = (jnp.arange(seq_len, dtype=jnp.int32)[None, :] < lengths[:, None] - 1)
    counts = (lengths - 1).astype(f32)
    column = jnp.arange(vocab, dtype=jnp.int32)
    here = (ids.reshape(-1)[:, None] == column).astype(bf16)
    there = (next_ids.reshape(-1)[:, None] == column) & live.reshape(-1)[:, None]
    gap = prior_logp - agent_logp
    gap_hi = gap.astype(bf16)
    gap_lo = (gap - gap_hi.astype(f32)).astype(bf16)
    looked = dot(here, gap_hi, ((1,), (0,))) + dot(here, gap_lo, ((1,), (0,)))
    term = jnp.sum(jnp.where(there, looked, 0.0).reshape(seqs, seq_len * vocab), axis=1)
    margin = term / counts + SIGMA_WEIGHT * scores.astype(f32) / LEVELS
    factor = 2.0 * margin / counts

    token_factor = jnp.repeat(factor, seq_len)
    weighted = jnp.where(there, token_factor[:, None], 0.0)
    weighted_hi = weighted.astype(bf16)
    weighted_lo = (weighted - weighted_hi.astype(f32)).astype(bf16)
    pair_sum = dot(here, weighted_hi, ((0,), (0,))) + dot(here, weighted_lo, ((0,), (0,)))
    logit_grad = jnp.sum(pair_sum, axis=1, keepdims=True) * jnp.exp(agent_logp) - pair_sum
    scaled = dot(logit_grad.astype(bf16), head_weight, ((1,), (1,))) * final_gain
    hidden_grad = (
        inverse * scaled
        - hidden * inverse * inverse * inverse * jnp.mean(hidden * scaled, axis=-1, keepdims=True)
    ).astype(bf16)
    latent_grad = dot(hidden_grad, up, ((1,), (0,))).astype(bf16)
    share = width // (segments * groups * replicas)
    first = ((segment_pos * groups + group_pos) * replicas + rep_pos) * share
    own_unit = lax.dynamic_slice_in_dim(unit, first, share, 1)
    own_grad = lax.dynamic_slice_in_dim(hidden_grad, first, share, 1)
    return (
        dot(own_unit, latent_grad, ((0,), (0,))),
        dot(own_grad, latent, ((0,), (0,))),
    )


def solution(mesh):
    placed = (
        P("fsdp", None),
        P("fsdp"),
        P("fsdp"),
        P(),
        P("segment", None, "rep"),
        P("segment", None),
        P(),
        P(),
        P("fsdp", None),
        P("fsdp", None),
    )
    spread = P(("segment", "fsdp", "rep"), None)
    return jax.shard_map(
        on_device, mesh=mesh, in_specs=placed, out_specs=(spread, spread), check_vma=False
    )
```

```python
import functools

import jax
import jax.numpy as jnp
from jax import lax
from jax.experimental import pallas as pl
from jax.experimental.pallas import tpu as pltpu
from jax.sharding import PartitionSpec as P

LEVELS = 64
EPSILON = 1e-05
SIGMA_WEIGHT = 2.0
MESH = pl.DeviceIdType.MESH

bf16 = jnp.bfloat16
f32 = jnp.float32
CHUNK = 256


def dot(a, b, dims=((1,), (0,)), precision=None):
    return lax.dot_general(a, b, (dims, ((), ())), precision=precision, preferred_element_type=f32)


def exact(a, b, dims=((1,), (0,))):
    return dot(a, b, dims, lax.Precision.HIGHEST)


def halves(a):
    high = a.astype(bf16)
    return high, (a - high.astype(f32)).astype(bf16)


def log_softmax(logits):
    shifted = logits - jnp.max(logits, axis=-1, keepdims=True)
    return shifted - jnp.log(jnp.sum(jnp.exp(shifted), axis=-1, keepdims=True))


def kernel(
    sizes,
    pack_ref,
    embed_ref,
    gain_ref,
    final_gain_ref,
    head_ref,
    down_ref,
    up_ref,
    embed_share_ref,
    head_share_ref,
    gain_share_ref,
    weight_hbm,
    down_out,
    up_out,
    weight,
    x_buf,
    normed,
    out_buf,
    tokens,
    part,
    from_z,
    gathered,
    up_share,
    pair_count,
    exchange,
    terms,
    factor_buf,
    lat_buf,
    wide_buf,
    rank_buf,
    agent_terms,
    hidden_share,
    weight_sem,
    x_send,
    x_recv,
    tok_send,
    tok_recv,
    z_send,
    z_recv,
    g_send,
    g_recv,
    u_send,
    u_recv,
    e_send,
    e_recv,
    t_send,
    t_recv,
):
    S, G, R = sizes
    seg, grp, rep = lax.axis_index("segment"), lax.axis_index("fsdp"), lax.axis_index("rep")
    vocab, width = embed_ref.shape
    rank = up_ref.shape[1]
    depth = up_ref.shape[0]
    rows = x_buf.shape[1]
    blocks = vocab // rows
    cohort = grp // blocks
    block = grp - cohort * blocks
    chunks = out_buf.shape[0]
    teams = S * R
    team = seg * R + rep
    vr, rr = vocab // teams, rank // teams
    share = up_share.shape[0]
    seqs = pair_count.shape[0]
    group_seqs = seqs // G

    def remote(src, dst, send, recv, device):
        return pltpu.make_async_remote_copy(
            src_ref=src, dst_ref=dst, send_sem=send, recv_sem=recv, device_id=device, device_id_type=MESH
        )

    def weight_copy(j):
        cols = pl.ds(pl.multiple_of(j * CHUNK, CHUNK), CHUNK)
        return pltpu.make_async_copy(weight_hbm.at[0, :, cols], weight.at[j], weight_sem.at[j])

    def start_weight(j, carry):
        weight_copy(j).start()
        return carry

    lax.fori_loop(0, chunks, start_weight, 0)

    barrier = pltpu.get_barrier_semaphore()
    for a in range(S):
        for b in range(G):
            for c in range(R):
                if a + b + c:
                    other = (lax.rem(seg + a, S), lax.rem(grp + b, G), lax.rem(rep + c, R))
                    pl.semaphore_signal(barrier, inc=1, device_id=other, device_id_type=MESH)
    pl.semaphore_wait(barrier, S * G * R - 1)

    tokens[grp] = pack_ref[...]
    token_copies = [
        remote(
            pack_ref, tokens.at[grp], tok_send.at[b - 1], tok_recv.at[b - 1], (seg, lax.rem(grp + b, G), rep)
        )
        for b in range(1, G)
    ]
    for copy in token_copies:
        copy.start()

    def x_copy(j, to):
        return remote(
            out_buf.at[j],
            x_buf.at[rep * chunks + j],
            x_send.at[j, to],
            x_recv.at[rep * chunks + j],
            (lax.rem(seg + 1, S), grp, to),
        )

    def x_arrival(c):
        return remote(out_buf.at[0], x_buf.at[c], x_send.at[0, 0], x_recv.at[c], (lax.rem(seg + 1, S), grp, rep))

    def section(first, last):
        total = jnp.zeros((rows, CHUNK), f32)
        for c in range(R * chunks):
            if first:
                x = embed_ref[pl.ds(pl.multiple_of(block * rows, rows), rows), c * CHUNK : (c + 1) * CHUNK]
                x_buf[c] = x
            else:
                x_arrival(c).wait_recv()
                x = x_buf[c]
            x = x.astype(f32)
            total = total + x * x
        scale = lax.rsqrt(jnp.sum(total, axis=-1, keepdims=True) / width + EPSILON)
        for c in range(R * chunks):
            cols = slice(c * CHUNK, (c + 1) * CHUNK)
            normed[:, cols] = (x_buf[c].astype(f32) * scale * gain_ref[:, cols]).astype(bf16)

        def one(j, carry):
            weight_copy(j).wait()
            update = dot(normed[...], weight[j])
            out_buf[j] = (x_buf[rep * chunks + j].astype(f32) + update).astype(bf16)
            for to in range(R):
                if last is None:
                    x_copy(j, to).start()
                else:

                    @pl.when(jnp.logical_not(last))
                    def _():
                        x_copy(j, to).start()

            return carry

        lax.fori_loop(0, chunks, one, 0)

    def drain_sends():
        def one(j, carry):
            for to in range(R):
                x_copy(j, to).wait_send()
            return carry

        lax.fori_loop(0, chunks, one, 0)

    @pl.when(seg == 0)
    def _():
        section(True, None)

    features = pl.ds(pl.multiple_of(grp * depth, depth), depth)
    table = embed_ref[...].astype(f32)
    square = jnp.sum(table * table, axis=-1, keepdims=True)
    unit_scale = lax.rsqrt(square / width + EPSILON)
    own_table = embed_ref[:, features]
    up = up_ref[...]
    unit_own = (own_table.astype(f32) * unit_scale).astype(bf16)
    part[:, 0:vr, :] = dot(own_table, up).reshape(teams, vr, rank)
    head_own = head_ref[features, :].astype(f32).T * final_gain_ref[:, features]
    high, low = halves(head_own)
    part[:, vr : 2 * vr, :] = (dot(high, up) + dot(low, up)).reshape(teams, vr, rank)
    part[:, 2 * vr : 3 * vr, :] = dot(unit_own, down_ref[...]).reshape(teams, vr, rank)
    part[:, 3 * vr :, :] = dot(up, up, ((0,), (0,))).reshape(teams, rr, rank)

    z_copies = [
        remote(
            part.at[team], from_z.at[b - 1], z_send.at[b - 1], z_recv.at[b - 1], (seg, lax.rem(grp + b, G), rep)
        )
        for b in range(1, G)
    ]
    for copy in z_copies:
        copy.start()

    def owner(g):
        return (seg * G + g) // S

    def share_row(g):
        flat = (seg * G + g) * R + rep
        return pl.multiple_of((flat - owner(g) * teams) * share, share)

    def up_copy(b):
        target = lax.rem(grp + b, G)
        return remote(
            up_ref.at[pl.ds(share_row(target), share), :],
            up_share,
            u_send.at[b - 1],
            u_recv.at[0],
            (seg, target, rep),
        )

    for b in range(1, G):

        @pl.when(owner(lax.rem(grp + b, G)) == grp)
        def _():
            up_copy(b).start()

    @pl.when(owner(grp) == grp)
    def _():
        up_share[...] = up_ref[pl.ds(share_row(grp), share), :]

    @pl.when(owner(grp) != grp)
    def _():
        remote(up_share, up_share, u_send.at[0], u_recv.at[0], (seg, lax.rem(grp + 1, G), rep)).wait_recv()

    for copy in z_copies:
        copy.wait_recv()
    total = part[team]
    for b in range(1, G):
        total = total + from_z[b - 1]
    gathered[team] = total
    g_copies = []
    for a in range(S):
        for c in range(R):
            if a + c:
                k = a * R + c - 1
                g_copies.append(
                    remote(
                        gathered.at[team],
                        gathered.at[team],
                        g_send.at[k],
                        g_recv.at[k],
                        (lax.rem(seg + a, S), grp, lax.rem(rep + c, R)),
                    )
                )
    for copy in g_copies:
        copy.start()

    @pl.when(seg == 1)
    def _():
        section(False, None)

    for copy in token_copies:
        copy.wait_recv()
    ids_iota = lax.broadcasted_iota(jnp.int32, (vocab, tokens.shape[2]), 0)

    def count(g, carry):
        for i in range(group_seqs):
            here = (tokens[g, i : i + 1, :] == ids_iota).astype(bf16)
            there = (tokens[g, group_seqs + i : group_seqs + i + 1, :] == ids_iota).astype(bf16)
            pair_count[g * group_seqs + i] = dot(here, there, ((1,), (1,)))
        return carry

    lax.fori_loop(0, G, count, 0)

    table_gain = embed_ref[...].astype(f32) * final_gain_ref[...]
    high, low = halves(table_gain)
    table_logits = dot(high, head_ref[...]) + dot(low, head_ref[...])
    for copy in g_copies:
        copy.wait_recv()
    table_up = gathered[:, 0:vr, :].reshape(vocab, rank)
    head_up = gathered[:, vr : 2 * vr, :].reshape(vocab, rank)
    latent = gathered[:, 2 * vr : 3 * vr, :].reshape(vocab, rank).astype(bf16)
    up_up = gathered[:, 3 * vr :, :].reshape(rank, rank)
    lat_buf[...] = latent
    latent_wide = latent.astype(f32)
    lat_up = exact(latent_wide, up_up)
    hidden_square = square + jnp.sum(latent_wide * (2.0 * table_up + lat_up), axis=-1, keepdims=True)
    inverse = lax.rsqrt(hidden_square / width + EPSILON)
    raw_logits = table_logits + exact(latent_wide, head_up, ((1,), (1,)))
    agent_logp = log_softmax(inverse * raw_logits)
    rank_buf[0] = head_up
    rank_buf[1] = table_up + lat_up
    wide_buf[0] = jnp.broadcast_to(inverse, (vocab, vocab))
    wide_buf[1] = raw_logits
    wide_buf[2] = jnp.exp(agent_logp)
    hidden_share[...] = embed_share_ref[...].astype(f32) + dot(latent, up_share[...], ((1,), (1,)))
    wide_buf[3] = agent_logp

    def agent_term(g, carry):
        first = pl.multiple_of(g * group_seqs, group_seqs)
        agent_terms[pl.ds(first, group_seqs), :] = jnp.sum(
            pair_count[pl.ds(first, group_seqs)] * wide_buf[3][None], axis=1
        )
        return carry

    lax.fori_loop(0, G, agent_term, 0)

    @pl.when(seg >= 2)
    def _():
        section(False, seg == S - 1)

    def term_copy(a, b):
        target = cohort * blocks + lax.rem(block + b, blocks)
        k = a * blocks + b - 1
        return remote(
            terms.at[block], terms.at[block], t_send.at[k], t_recv.at[b], (lax.rem(seg + a, S), target, rep)
        )

    @pl.when(seg == S - 1)
    def _():
        logits = jnp.zeros((rows, vocab), f32)
        squares = jnp.zeros((rows, CHUNK), f32)
        for j in range(chunks):
            cols = pl.ds(pl.multiple_of((rep * chunks + j) * CHUNK, CHUNK), CHUNK)
            x = out_buf[j].astype(f32)
            squares = squares + x * x
            logits = logits + dot((x * final_gain_ref[:, cols]).astype(bf16), head_ref[cols, :])
        exchange[0, 0] = logits
        exchange[0, 1] = jnp.broadcast_to(jnp.sum(squares, axis=-1, keepdims=True), (rows, vocab))
        e_copies = [
            remote(exchange.at[0], exchange.at[c], e_send.at[c - 1], e_recv.at[c - 1], (seg, grp, lax.rem(rep + c, R)))
            for c in range(1, R)
        ]
        for copy in e_copies:
            copy.start()
        for copy in e_copies:
            copy.wait_recv()
        logits = exchange[0, 0]
        squares = exchange[0, 1]
        for c in range(1, R):
            logits = logits + exchange[c, 0]
            squares = squares + exchange[c, 1]
        exchange_logp = log_softmax(logits * lax.rsqrt(squares / width + EPSILON))
        exchange[R, 0] = exchange_logp
        own_rows = pl.ds(pl.multiple_of(block * rows, rows), rows)

        def prior_term(g, carry):
            first = pl.multiple_of(g * group_seqs, group_seqs)
            terms[block, pl.ds(first, group_seqs), :] = jnp.sum(
                pair_count[pl.ds(first, group_seqs), own_rows, :] * exchange[R, 0][None], axis=1
            )
            return carry

        lax.fori_loop(0, G, prior_term, 0)
        for a in range(S):
            for b in range(blocks):
                if a + b:
                    term_copy(a, b).start()
        for copy in e_copies:
            copy.wait_send()

    for b in range(blocks):

        def wait_term():
            came = lax.rem(block + blocks - b, blocks)
            remote(
                terms.at[came], terms.at[came], t_send.at[0], t_recv.at[b], (lax.rem(seg + 1, S), grp, rep)
            ).wait_recv()

        if b == 0:
            pl.when(seg != S - 1)(wait_term)
        else:
            wait_term()

    difference = -agent_terms[...]
    for b in range(blocks):
        difference = difference + terms[b]
    counts = tokens[:, 2 * group_seqs : 3 * group_seqs, :].reshape(seqs, -1).astype(f32)
    scores = tokens[:, 3 * group_seqs :, :].reshape(seqs, -1).astype(f32)
    margin = jnp.sum(difference, axis=-1, keepdims=True) / counts + SIGMA_WEIGHT * scores / LEVELS
    factor_buf[...] = 2.0 * margin / counts

    def weigh(i, total):
        for k in range(4):
            total = total + pair_count[i * 4 + k] * factor_buf[pl.ds(i * 4 + k, 1), :]
        return total

    weighted = lax.fori_loop(0, seqs // 4, weigh, jnp.zeros((vocab, vocab), f32))
    logit_grad = jnp.sum(weighted, axis=-1, keepdims=True) * wide_buf[2] - weighted
    inverse = wide_buf[0][:, 0:1]
    mean = jnp.sum(logit_grad * wide_buf[1], axis=-1, keepdims=True) / width
    pull = inverse * inverse * inverse * mean
    latent_grad = (inverse * exact(logit_grad, rank_buf[0]) - pull * rank_buf[1]).astype(bf16)
    wide_share = embed_share_ref[...].astype(f32)
    table = embed_ref[...].astype(f32)
    unit_scale = lax.rsqrt(jnp.sum(table * table, axis=-1, keepdims=True) / width + EPSILON)
    unit_share = (wide_share * unit_scale).astype(bf16)
    down_out[...] = dot(unit_share, latent_grad, ((0,), (0,)))
    scaled = dot(logit_grad.astype(bf16), head_share_ref[...], ((1,), (1,))) * gain_share_ref[...]
    hidden_grad = (inverse * scaled - hidden_share[...] * pull).astype(bf16)
    up_out[...] = dot(hidden_grad, lat_buf[...], ((0,), (0,)))

    for copy in token_copies + z_copies + g_copies:
        copy.wait_send()
    for b in range(1, G):

        @pl.when(owner(lax.rem(grp + b, G)) == grp)
        def _():
            up_copy(b).wait_send()

    @pl.when(seg != S - 1)
    def _():
        drain_sends()

    @pl.when(seg == S - 1)
    def _():
        for a in range(S):
            for b in range(blocks):
                if a + b:
                    term_copy(a, b).wait_send()


def on_device(
    token_ids,
    seq_lengths,
    quant_scores,
    embed_table,
    prior_weight,
    prior_gain,
    final_gain,
    head_weight,
    agent_down,
    agent_up,
):
    S, G, R = (lax.axis_size(a) for a in ("segment", "fsdp", "rep"))
    seg, grp, rep = (lax.axis_index(a) for a in ("segment", "fsdp", "rep"))
    vocab, width = embed_table.shape
    rank = agent_up.shape[1]
    group_seqs, seq_len = token_ids.shape
    seqs = group_seqs * G
    half = prior_weight.shape[2]
    chunks = half // CHUNK
    rows = max(16, vocab // G)
    blocks = vocab // rows
    teams = S * R
    vr, rr = vocab // teams, rank // teams
    share = width // (S * G * R)

    positions = jnp.arange(seq_len, dtype=jnp.int32)
    ahead = jnp.concatenate([token_ids[:, 1:], token_ids[:, :1]], axis=1)
    spread = lambda v: jnp.broadcast_to(v[:, None], (group_seqs, seq_len))
    pack = jnp.concatenate(
        [
            token_ids,
            jnp.where(positions[None, :] < seq_lengths[:, None] - 1, ahead, -1),
            spread(seq_lengths - 1),
            spread(quant_scores),
        ],
        axis=0,
    )
    first = ((seg * G + grp) * R + rep) * share
    embed_share = lax.dynamic_slice_in_dim(embed_table, first, share, 1)
    head_share = lax.dynamic_slice_in_dim(head_weight, first, share, 0)
    gain_share = lax.dynamic_slice_in_dim(final_gain, first, share, 0)[None]

    vmem = pl.BlockSpec(memory_space=pltpu.VMEM)
    dma = pltpu.SemaphoreType.DMA
    return pl.pallas_call(
        functools.partial(kernel, (S, G, R)),
        out_shape=[jax.ShapeDtypeStruct((share, rank), f32)] * 2,
        in_specs=[vmem] * 10 + [pl.BlockSpec(memory_space=pl.ANY)],
        out_specs=[vmem, vmem],
        scratch_shapes=[
            pltpu.VMEM((chunks, width, CHUNK), bf16),
            pltpu.VMEM((R * chunks, rows, CHUNK), bf16),
            pltpu.VMEM((rows, width), bf16),
            pltpu.VMEM((chunks, rows, CHUNK), bf16),
            pltpu.VMEM((G, 4 * group_seqs, seq_len), jnp.int32),
            pltpu.VMEM((teams, 3 * vr + rr, rank), f32),
            pltpu.VMEM((G - 1, 3 * vr + rr, rank), f32),
            pltpu.VMEM((teams, 3 * vr + rr, rank), f32),
            pltpu.VMEM((share, rank), bf16),
            pltpu.VMEM((seqs, vocab, vocab), f32),
            pltpu.VMEM((R + 1, 2, rows, vocab), f32),
            pltpu.VMEM((blocks, seqs, vocab), f32),
            pltpu.VMEM((seqs, vocab), f32),
            pltpu.VMEM((vocab, rank), bf16),
            pltpu.VMEM((4, vocab, vocab), f32),
            pltpu.VMEM((2, vocab, rank), f32),
            pltpu.VMEM((seqs, vocab), f32),
            pltpu.VMEM((vocab, share), f32),
            dma((chunks,)),
            dma((chunks, R)),
            dma((R * chunks,)),
            dma((G - 1,)),
            dma((G - 1,)),
            dma((G - 1,)),
            dma((G - 1,)),
            dma((teams - 1,)),
            dma((teams - 1,)),
            dma((G - 1,)),
            dma((1,)),
            dma((R - 1,)),
            dma((R - 1,)),
            dma((S * blocks - 1,)),
            dma((blocks,)),
        ],
        compiler_params=pltpu.CompilerParams(
            collective_id=0, has_side_effects=True, vmem_limit_bytes=56 * 1024 * 1024
        ),
    )(
        pack,
        embed_table,
        prior_gain,
        final_gain[None],
        head_weight,
        agent_down,
        agent_up,
        embed_share,
        head_share,
        gain_share,
        prior_weight,
    )


def solution(mesh):
    placed = (
        P("fsdp", None),
        P("fsdp"),
        P("fsdp"),
        P(),
        P("segment", None, "rep"),
        P("segment", None),
        P(),
        P(),
        P("fsdp", None),
        P("fsdp", None),
    )
    spread = P(("segment", "fsdp", "rep"), None)

    def run(*args):
        return tuple(on_device(*args))

    return jax.shard_map(run, mesh=mesh, in_specs=placed, out_specs=(spread, spread), check_vma=False)
```

```python
import functools

import jax
import jax.numpy as jnp
from jax import lax
from jax.experimental import pallas as pl
from jax.experimental.pallas import tpu as pltpu
from jax.sharding import PartitionSpec as P

LEVELS = 64
EPSILON = 1e-05
SIGMA_WEIGHT = 2.0
MESH = pl.DeviceIdType.MESH

bf16 = jnp.bfloat16
f32 = jnp.float32
CHUNK = 256


def dot(a, b, dims=((1,), (0,)), precision=None):
    return lax.dot_general(a, b, (dims, ((), ())), precision=precision, preferred_element_type=f32)


def exact(a, b, dims=((1,), (0,))):
    return dot(a, b, dims, lax.Precision.HIGHEST)


def halves(a):
    high = a.astype(bf16)
    return high, (a - high.astype(f32)).astype(bf16)


def log_softmax(logits):
    shifted = logits - jnp.max(logits, axis=-1, keepdims=True)
    return shifted - jnp.log(jnp.sum(jnp.exp(shifted), axis=-1, keepdims=True))


def kernel(
    sizes,
    ids_ref,
    length_ref,
    score_ref,
    embed_ref,
    gain_ref,
    final_gain_ref,
    head_ref,
    down_ref,
    up_ref,
    weight_hbm,
    down_out,
    up_out,
    weight,
    x_buf,
    normed,
    out_buf,
    tokens,
    part,
    from_z,
    gathered,
    up_share,
    pair_count,
    exchange,
    terms,
    factor_buf,
    lat_buf,
    wide_buf,
    head_up_buf,
    rank_buf,
    pack_ref,
    window_out,
    agent_terms,
    hidden_share,
    weight_sem,
    x_send,
    x_recv,
    tok_send,
    tok_recv,
    z_send,
    z_recv,
    g_send,
    g_recv,
    u_send,
    u_recv,
    e_send,
    e_recv,
    t_send,
    t_recv,
):
    S, G, R = sizes
    seg, grp, rep = lax.axis_index("segment"), lax.axis_index("fsdp"), lax.axis_index("rep")
    vocab, width = embed_ref.shape
    rank = up_ref.shape[1]
    depth = up_ref.shape[0]
    rows = x_buf.shape[1]
    blocks = vocab // rows
    cohort = grp // blocks
    block = grp - cohort * blocks
    chunks = out_buf.shape[0]
    teams = S * R
    team = seg * R + rep
    vr, rr = vocab // teams, rank // teams
    share = down_out.shape[0]
    window = up_share.shape[0]
    first = ((seg * G + grp) * R + rep) * share
    base = pl.multiple_of(first - lax.rem(first, window), window)
    window_cols = pl.ds(base, window)
    seqs = pair_count.shape[0]
    group_seqs = seqs // G

    def remote(src, dst, send, recv, device):
        return pltpu.make_async_remote_copy(
            src_ref=src, dst_ref=dst, send_sem=send, recv_sem=recv, device_id=device, device_id_type=MESH
        )

    def weight_copy(j):
        cols = pl.ds(pl.multiple_of(j * CHUNK, CHUNK), CHUNK)
        return pltpu.make_async_copy(weight_hbm.at[0, :, cols], weight.at[j], weight_sem.at[j])

    def start_weight(j, carry):
        weight_copy(j).start()
        return carry

    lax.fori_loop(0, chunks, start_weight, 0)

    barrier = pltpu.get_barrier_semaphore()
    for a in range(S):
        for b in range(G):
            for c in range(R):
                if a + b + c:
                    other = (lax.rem(seg + a, S), lax.rem(grp + b, G), lax.rem(rep + c, R))
                    pl.semaphore_signal(barrier, inc=1, device_id=other, device_id_type=MESH)

    def x_copy(j):
        c = rep * chunks + j
        return remote(out_buf.at[j], x_buf.at[c], x_send.at[j, 0], x_recv.at[c], (lax.rem(seg + 1, S), grp, rep))

    def x_arrival(c):
        return remote(
            out_buf.at[0], x_buf.at[c], x_send.at[0, 0], x_recv.at[c], (lax.rem(seg + 1, S), grp, rep)
        )

    def x_forward(j, k):
        c = rep * chunks + j
        return remote(x_buf.at[c], x_buf.at[c], x_send.at[j, k], x_recv.at[c], (seg, grp, lax.rem(rep + k, R)))

    def section(first, last):
        total = jnp.zeros((rows, CHUNK), f32)
        if first:
            for c in range(R * chunks):
                x = embed_ref[pl.ds(pl.multiple_of(block * rows, rows), rows), c * CHUNK : (c + 1) * CHUNK]
                x_buf[c] = x
                x = x.astype(f32)
                total = total + x * x
        else:
            for j in range(chunks):
                x_arrival(rep * chunks + j).wait_recv()
                for k in range(1, R):
                    x_forward(j, k).start()
                x = x_buf[rep * chunks + j].astype(f32)
                total = total + x * x
            for j in range(chunks):
                for k in range(1, R):
                    c = lax.rem(rep + k, R) * chunks + j
                    x_arrival(c).wait_recv()
                    x = x_buf[c].astype(f32)
                    total = total + x * x
        scale = lax.rsqrt(jnp.sum(total, axis=-1, keepdims=True) / width + EPSILON)
        for c in range(R * chunks):
            cols = slice(c * CHUNK, (c + 1) * CHUNK)
            normed[:, cols] = (x_buf[c].astype(f32) * scale * gain_ref[:, cols]).astype(bf16)

        def one(j, carry):
            weight_copy(j).wait()
            update = dot(normed[...], weight[j])
            out_buf[j] = (x_buf[rep * chunks + j].astype(f32) + update).astype(bf16)
            if last is None:
                x_copy(j).start()
            else:

                @pl.when(jnp.logical_not(last))
                def _():
                    x_copy(j).start()

            return carry

        lax.fori_loop(0, chunks, one, 0)

    def drain(copies):
        def one(j, carry):
            for copy in copies(j):
                copy.wait_send()
            return carry

        lax.fori_loop(0, chunks, one, 0)

    features = pl.ds(pl.multiple_of(grp * depth, depth), depth)
    table = embed_ref[...].astype(f32)
    square = jnp.sum(table * table, axis=-1, keepdims=True)
    unit_scale = lax.rsqrt(square / width + EPSILON)
    own_table = embed_ref[:, features]
    up = up_ref[...]
    unit_own = (own_table.astype(f32) * unit_scale).astype(bf16)
    part[:, 0:vr, :] = dot(own_table, up).reshape(teams, vr, rank)
    head_own = head_ref[features, :].astype(f32).T * final_gain_ref[:, features]
    high, low = halves(head_own)
    part[:, vr : 2 * vr, :] = (dot(high, up) + dot(low, up)).reshape(teams, vr, rank)
    part[:, 2 * vr : 3 * vr, :] = dot(unit_own, down_ref[...]).reshape(teams, vr, rank)
    part[:, 3 * vr :, :] = dot(up, up, ((0,), (0,))).reshape(teams, rr, rank)

    pl.semaphore_wait(barrier, S * G * R - 1)
    position = lax.broadcasted_iota(jnp.int32, (1, ids_ref.shape[1]), 1)
    ids = ids_ref[...]
    pack_ref[0:group_seqs, :] = ids
    ahead = pltpu.roll(ids, ids.shape[1] - 1, 1)
    for i in range(group_seqs):
        count_now = length_ref[i] - 1
        at = group_seqs + i
        pack_ref[at : at + 1, :] = jnp.where(position < count_now, ahead[i : i + 1, :], -1)
        at = at + group_seqs
        pack_ref[at : at + 1, :] = jnp.zeros_like(position) + count_now
        at = at + group_seqs
        pack_ref[at : at + 1, :] = jnp.zeros_like(position) + score_ref[i]
    tokens[grp] = pack_ref[...]
    token_copies = [
        remote(
            pack_ref, tokens.at[grp], tok_send.at[b - 1], tok_recv.at[b - 1], (seg, lax.rem(grp + b, G), rep)
        )
        for b in range(1, G)
    ]
    for copy in token_copies:
        copy.start()

    z_copies = [
        remote(
            part.at[team], from_z.at[b - 1], z_send.at[b - 1], z_recv.at[b - 1], (seg, lax.rem(grp + b, G), rep)
        )
        for b in range(1, G)
    ]
    for copy in z_copies:
        copy.start()

    def owner(g):
        return (seg * G + g) // S

    def share_row(g):
        flat = (seg * G + g) * R + rep
        row = (flat - owner(g) * teams) * share
        return pl.multiple_of(row - lax.rem(row, window), window)

    def up_copy(b):
        target = lax.rem(grp + b, G)
        return remote(
            up_ref.at[pl.ds(share_row(target), window), :],
            up_share,
            u_send.at[b - 1],
            u_recv.at[0],
            (seg, target, rep),
        )

    for b in range(1, G):

        @pl.when(owner(lax.rem(grp + b, G)) == grp)
        def _():
            up_copy(b).start()

    @pl.when(owner(grp) == grp)
    def _():
        up_share[...] = up_ref[pl.ds(share_row(grp), window), :]

    @pl.when(owner(grp) != grp)
    def _():
        remote(up_share, up_share, u_send.at[0], u_recv.at[0], (seg, lax.rem(grp + 1, G), rep)).wait_recv()

    @pl.when(seg == 0)
    def _():
        section(True, None)

    for copy in z_copies:
        copy.wait_recv()
    total = part[team]
    for b in range(1, G):
        total = total + from_z[b - 1]
    gathered[team] = total.astype(bf16)
    g_copies = []
    for a in range(S):
        for c in range(R):
            if a + c:
                k = a * R + c - 1
                g_copies.append(
                    remote(
                        gathered.at[team],
                        gathered.at[team],
                        g_send.at[k],
                        g_recv.at[k],
                        (lax.rem(seg + a, S), grp, lax.rem(rep + c, R)),
                    )
                )
    for copy in g_copies:
        copy.start()

    @pl.when(seg == 1)
    def _():
        section(False, None)

    for copy in token_copies:
        copy.wait_recv()
    ids_iota = lax.broadcasted_iota(jnp.int32, (vocab, tokens.shape[2]), 0)

    def count(g, carry):
        for i in range(group_seqs):
            here = (tokens[g, i : i + 1, :] == ids_iota).astype(bf16)
            there = (tokens[g, group_seqs + i : group_seqs + i + 1, :] == ids_iota).astype(bf16)
            pair_count[g * group_seqs + i] = dot(here, there, ((1,), (1,)))
        return carry

    lax.fori_loop(0, G, count, 0)

    table_gain = embed_ref[...].astype(f32) * final_gain_ref[...]
    high, low = halves(table_gain)
    table_logits = dot(high, head_ref[...]) + dot(low, head_ref[...])
    for copy in g_copies:
        copy.wait_recv()
    table_up = gathered[:, 0:vr, :].reshape(vocab, rank).astype(f32)
    head_up = gathered[:, vr : 2 * vr, :].reshape(vocab, rank)
    latent = gathered[:, 2 * vr : 3 * vr, :].reshape(vocab, rank)
    up_up = gathered[:, 3 * vr :, :].reshape(rank, rank)
    lat_buf[...] = latent
    latent_wide = latent.astype(f32)
    lat_up = dot(latent, up_up)
    hidden_square = square + jnp.sum(latent_wide * (2.0 * table_up + lat_up), axis=-1, keepdims=True)
    inverse = lax.rsqrt(hidden_square / width + EPSILON)
    raw_logits = table_logits + dot(latent, head_up, ((1,), (1,)))
    agent_logp = log_softmax(inverse * raw_logits)
    head_up_buf[...] = head_up
    rank_buf[...] = table_up + lat_up
    wide_buf[0] = jnp.broadcast_to(inverse, (vocab, vocab))
    wide_buf[1] = raw_logits
    wide_buf[2] = jnp.exp(agent_logp)
    hidden_share[...] = embed_ref[:, window_cols].astype(f32) + dot(latent, up_share[...], ((1,), (1,)))
    wide_buf[3] = agent_logp

    def agent_term(g, carry):
        first = pl.multiple_of(g * group_seqs, group_seqs)
        agent_terms[pl.ds(first, group_seqs), :] = jnp.sum(
            pair_count[pl.ds(first, group_seqs)] * wide_buf[3][None], axis=1
        )
        return carry

    lax.fori_loop(0, G, agent_term, 0)

    @pl.when(seg >= 2)
    def _():
        section(False, seg == S - 1)

    def term_copy(a, b):
        target = cohort * blocks + lax.rem(block + b, blocks)
        k = a * blocks + b - 1
        return remote(
            terms.at[block], terms.at[block], t_send.at[k], t_recv.at[b], (lax.rem(seg + a, S), target, rep)
        )

    @pl.when(seg == S - 1)
    def _():
        logits = jnp.zeros((rows, vocab), f32)
        squares = jnp.zeros((rows, CHUNK), f32)
        for j in range(chunks):
            cols = pl.ds(pl.multiple_of((rep * chunks + j) * CHUNK, CHUNK), CHUNK)
            x = out_buf[j].astype(f32)
            squares = squares + x * x
            logits = logits + dot((x * final_gain_ref[:, cols]).astype(bf16), head_ref[cols, :])
        exchange[0, 0] = logits
        exchange[0, 1] = jnp.broadcast_to(jnp.sum(squares, axis=-1, keepdims=True), (rows, vocab))
        e_copies = [
            remote(exchange.at[0], exchange.at[c], e_send.at[c - 1], e_recv.at[c - 1], (seg, grp, lax.rem(rep + c, R)))
            for c in range(1, R)
        ]
        for copy in e_copies:
            copy.start()
        for copy in e_copies:
            copy.wait_recv()
        logits = exchange[0, 0]
        squares = exchange[0, 1]
        for c in range(1, R):
            logits = logits + exchange[c, 0]
            squares = squares + exchange[c, 1]
        exchange_logp = log_softmax(logits * lax.rsqrt(squares / width + EPSILON))
        exchange[R, 0] = exchange_logp
        own_rows = pl.ds(pl.multiple_of(block * rows, rows), rows)

        def prior_term(g, carry):
            first = pl.multiple_of(g * group_seqs, group_seqs)
            terms[block, pl.ds(first, group_seqs), :] = jnp.sum(
                pair_count[pl.ds(first, group_seqs), own_rows, :] * exchange[R, 0][None], axis=1
            )
            return carry

        lax.fori_loop(0, G, prior_term, 0)
        for a in range(S):
            for b in range(blocks):
                if a + b:
                    term_copy(a, b).start()
        for copy in e_copies:
            copy.wait_send()

    for b in range(blocks):

        def wait_term():
            came = lax.rem(block + blocks - b, blocks)
            remote(
                terms.at[came], terms.at[came], t_send.at[0], t_recv.at[b], (lax.rem(seg + 1, S), grp, rep)
            ).wait_recv()

        if b == 0:
            pl.when(seg != S - 1)(wait_term)
        else:
            wait_term()

    difference = -agent_terms[...]
    for b in range(blocks):
        difference = difference + terms[b]
    counts = tokens[:, 2 * group_seqs : 3 * group_seqs, :].reshape(seqs, -1).astype(f32)
    scores = tokens[:, 3 * group_seqs :, :].reshape(seqs, -1).astype(f32)
    margin = jnp.sum(difference, axis=-1, keepdims=True) / counts + SIGMA_WEIGHT * scores / LEVELS
    factor_buf[...] = 2.0 * margin / counts

    def weigh(i, total):
        for k in range(4):
            total = total + pair_count[i * 4 + k] * factor_buf[pl.ds(i * 4 + k, 1), :]
        return total

    weighted = lax.fori_loop(0, seqs // 4, weigh, jnp.zeros((vocab, vocab), f32))
    logit_grad = jnp.sum(weighted, axis=-1, keepdims=True) * wide_buf[2] - weighted
    inverse = wide_buf[0][:, 0:1]
    mean = jnp.sum(logit_grad * wide_buf[1], axis=-1, keepdims=True) / width
    pull = inverse * inverse * inverse * mean
    high, low = halves(logit_grad)
    pulled = dot(high, head_up_buf[...]) + dot(low, head_up_buf[...])
    latent_grad = (inverse * pulled - pull * rank_buf[...]).astype(bf16)
    wide_share = embed_ref[:, window_cols].astype(f32)
    table = embed_ref[...].astype(f32)
    unit_scale = lax.rsqrt(jnp.sum(table * table, axis=-1, keepdims=True) / width + EPSILON)
    unit_share = (wide_share * unit_scale).astype(bf16)
    down_share = dot(unit_share, latent_grad, ((0,), (0,)))
    scaled = dot(logit_grad.astype(bf16), head_ref[window_cols, :], ((1,), (1,))) * final_gain_ref[:, window_cols]
    hidden_grad = (inverse * scaled - hidden_share[...] * pull).astype(bf16)
    up_grad = dot(hidden_grad, lat_buf[...], ((0,), (0,)))
    if window == share:
        down_out[...] = down_share
        up_out[...] = up_grad
    else:
        window_out[0] = down_share
        window_out[1] = up_grad
        within = pl.ds(pl.multiple_of(first - base, share), share)
        down_out[...] = window_out[0, within, :]
        up_out[...] = window_out[1, within, :]

    for copy in token_copies + z_copies + g_copies:
        copy.wait_send()
    for b in range(1, G):

        @pl.when(owner(lax.rem(grp + b, G)) == grp)
        def _():
            up_copy(b).wait_send()

    @pl.when(seg != S - 1)
    def _():
        drain(lambda j: [x_copy(j)])

    @pl.when(seg != 0)
    def _():
        drain(lambda j: [x_forward(j, k) for k in range(1, R)])

    @pl.when(seg == S - 1)
    def _():
        for a in range(S):
            for b in range(blocks):
                if a + b:
                    term_copy(a, b).wait_send()


def on_device(
    token_ids,
    seq_lengths,
    quant_scores,
    embed_table,
    prior_weight,
    prior_gain,
    final_gain,
    head_weight,
    agent_down,
    agent_up,
):
    S, G, R = (lax.axis_size(a) for a in ("segment", "fsdp", "rep"))
    vocab, width = embed_table.shape
    rank = agent_up.shape[1]
    group_seqs, seq_len = token_ids.shape
    seqs = group_seqs * G
    half = prior_weight.shape[2]
    chunks = half // CHUNK
    rows = max(16, vocab // G)
    blocks = vocab // rows
    teams = S * R
    vr, rr = vocab // teams, rank // teams
    share = width // (S * G * R)
    window = max(share, 128)

    smem = pl.BlockSpec(memory_space=pltpu.SMEM)
    vmem = pl.BlockSpec(memory_space=pltpu.VMEM)
    dma = pltpu.SemaphoreType.DMA
    return pl.pallas_call(
        functools.partial(kernel, (S, G, R)),
        out_shape=[jax.ShapeDtypeStruct((share, rank), f32)] * 2,
        in_specs=[vmem, smem, smem] + [vmem] * 6 + [pl.BlockSpec(memory_space=pl.ANY)],
        out_specs=[vmem, vmem],
        scratch_shapes=[
            pltpu.VMEM((chunks, width, CHUNK), bf16),
            pltpu.VMEM((R * chunks, rows, CHUNK), bf16),
            pltpu.VMEM((rows, width), bf16),
            pltpu.VMEM((chunks, rows, CHUNK), bf16),
            pltpu.VMEM((G, 4 * group_seqs, seq_len), jnp.int32),
            pltpu.VMEM((teams, 3 * vr + rr, rank), f32),
            pltpu.VMEM((G - 1, 3 * vr + rr, rank), f32),
            pltpu.VMEM((teams, 3 * vr + rr, rank), bf16),
            pltpu.VMEM((window, rank), bf16),
            pltpu.VMEM((seqs, vocab, vocab), f32),
            pltpu.VMEM((R + 1, 2, rows, vocab), f32),
            pltpu.VMEM((blocks, seqs, vocab), f32),
            pltpu.VMEM((seqs, vocab), f32),
            pltpu.VMEM((vocab, rank), bf16),
            pltpu.VMEM((4, vocab, vocab), f32),
            pltpu.VMEM((vocab, rank), bf16),
            pltpu.VMEM((vocab, rank), f32),
            pltpu.VMEM((4 * group_seqs, seq_len), jnp.int32),
            pltpu.VMEM((2, window, rank), f32),
            pltpu.VMEM((seqs, vocab), f32),
            pltpu.VMEM((vocab, window), f32),
            dma((chunks,)),
            dma((chunks, R)),
            dma((R * chunks,)),
            dma((G - 1,)),
            dma((G - 1,)),
            dma((G - 1,)),
            dma((G - 1,)),
            dma((teams - 1,)),
            dma((teams - 1,)),
            dma((G - 1,)),
            dma((1,)),
            dma((R - 1,)),
            dma((R - 1,)),
            dma((S * blocks - 1,)),
            dma((blocks,)),
        ],
        compiler_params=pltpu.CompilerParams(
            collective_id=0, has_side_effects=True, vmem_limit_bytes=56 * 1024 * 1024
        ),
    )(
        token_ids,
        seq_lengths,
        quant_scores,
        embed_table,
        prior_gain,
        final_gain[None],
        head_weight,
        agent_down,
        agent_up,
        prior_weight,
    )


def solution(mesh):
    placed = (
        P("fsdp", None),
        P("fsdp"),
        P("fsdp"),
        P(),
        P("segment", None, "rep"),
        P("segment", None),
        P(),
        P(),
        P("fsdp", None),
        P("fsdp", None),
    )
    spread = P(("segment", "fsdp", "rep"), None)

    def run(*args):
        return tuple(on_device(*args))

    return jax.shard_map(run, mesh=mesh, in_specs=placed, out_specs=(spread, spread), check_vma=False)
```
